1024 devices in a mesh: row: 64 (over z_hi, x, y), col: 16 (over z_lo, core).
Axes of the slice: x: 4, y: 8, z: 16 (z_hi: 2, z_lo: 8; z = z_hi * 8 + z_lo), core: 2. Of those that a mesh axis runs over, the one named last changes fastest.
Arguments:
- x_start: float32 [8, 131072], P(None, ('row', 'col')), may hold values from -0.75 to 0.75
- p_start: float32 [8, 131072], P(None, ('row', 'col')), may hold values from -0.75 to 0.75
- blocks: bfloat16 [64, 16, 96, 128, 128], P('row', 'col'), may hold values from -0.0546875 to 0.0546875
- block_in_row: int32 [64, 16, 96], P('row', 'col'), may hold values from 0 to 15, as said below
- col_block: int32 [64, 16, 96], P('row', 'col'), may hold values from 0 to 63
- coefs: float32 [2, 24, 8], replicated, may hold values from -3 to 3
Outputs:
- states: float32 [8, 131072], P(None, ('row', 'col'))
The draws below stay inside these ranges and needn't reach their ends.
Inputs may be any that keep to these rules, and one draw needn't show every extreme that they name: Every stored block lies on or above the block diagonal: col_block * 16 + c >= r * 16 + block_in_row on device (r, c).
All inputs are finite; a program needn't handle non-finite values.
Results may differ from the reference program's by a relative error of at most 0.0034.
Values may be sent and summed in bfloat16 or wider, within the bound.
A program may use at most 32 MiB of HBM per device.

```python
import jax
import jax.numpy as jnp
from jax import lax

STATES_K = 8
BLOCK = 128
NNZ = 96
ITERS = 2
SECTOR_STATES = 131072
N_ROW = 64
N_COL = 16


def triangle_pairs(key):
    first, second = jax.random.split(key)
    shape = (N_ROW, N_COL, NNZ)
    rowpos = jax.random.randint(first, shape, 0, N_COL, dtype=jnp.int32)
    group_r = jnp.arange(N_ROW, dtype=jnp.int32)[:, None, None]
    group_c = jnp.arange(N_COL, dtype=jnp.int32)[None, :, None]
    lowest = -((group_c - group_r * N_COL - rowpos) // N_COL)
    rowpos = jnp.where(lowest > N_ROW - 1, group_c + jnp.zeros_like(rowpos), rowpos)
    lowest = -((group_c - group_r * N_COL - rowpos) // N_COL)
    lowest = jnp.maximum(lowest, 0)
    spread = N_ROW - lowest
    raw = jax.random.randint(second, shape, 0, 1048576, dtype=jnp.int32)
    colpos = lowest + raw % spread
    return (rowpos.astype(jnp.int32), colpos.astype(jnp.int32))


def draw_block_in_row(key, part):
    pairs = triangle_pairs(key)
    return pairs[0]


def draw_col_block(key, part):
    pairs = triangle_pairs(key)
    return pairs[1]


def shard_levels(rng, extent, cuts, low, high):
    factor_of, own = 1.0, jax.random.fold_in(rng, 6)
    for position, blocks in cuts:
        draws = jnp.exp(jax.random.uniform(jax.random.fold_in(own, position), (blocks,), jnp.float32, low / len(cuts), high / len(cuts)))
        factor_of = factor_of * jnp.repeat(draws, extent[position] // blocks).reshape([-1 if axis == position else 1 for axis in range(len(extent))])
    return factor_of


def bell_draw(key, extent, deviation, limit, shards=(), kind=jnp.bfloat16):
    result = jax.random.normal(key, extent, jnp.float32) * deviation
    if len(shards) > 0:
        result = shard_levels(key, extent, shards, -0.22, 0.18) * result
    return jnp.clip(result, min=-limit, max=limit).astype(kind)


def setup_inputs(seed: int = 0) -> dict:
    seeds = jax.random.split(jax.random.key(seed), 7)
    x_start = bell_draw(seeds[0], (STATES_K, SECTOR_STATES), 0.05, 0.75, ((1, 1024),), jnp.float32)
    p_start = bell_draw(seeds[1], (STATES_K, SECTOR_STATES), 0.05, 0.75, ((1, 1024),), jnp.float32)
    blocks = bell_draw(seeds[2], (N_ROW, N_COL, NNZ, BLOCK, BLOCK), (NNZ * BLOCK) ** -0.5, 0.0546875, ((0, 64), (1, 16)))
    block_in_row = draw_block_in_row(jax.random.fold_in(seeds[6], 71), 0)
    col_block = draw_col_block(jax.random.fold_in(seeds[6], 71), 0)
    coefs = bell_draw(seeds[5], (ITERS, 3 * STATES_K, STATES_K), 0.5, 3.0, (), jnp.float32)
    return dict(x_start=x_start, p_start=p_start, blocks=blocks, block_in_row=block_in_row, col_block=col_block, coefs=coefs)


def apply_h(vec, blocks, block_in_row, col_block):
    rows = vec.shape[0]
    nblk = N_ROW * N_COL
    low = vec.astype(jnp.bfloat16).astype(jnp.float32).reshape(rows, nblk, BLOCK)
    cols_idx = jnp.arange(N_COL, dtype=jnp.int32)[:, None]

    def one_row(total, group):
        blk = blocks[group].reshape(-1, BLOCK, BLOCK).astype(jnp.float32)
        rblk = block_in_row[group]
        cblk = col_block[group]
        glob_i = (group * N_COL + rblk).reshape(-1).astype(jnp.int32)
        glob_j = (cblk * N_COL + cols_idx).reshape(-1).astype(jnp.int32)
        forward = jnp.einsum('mnb,nab->nma', low[:, glob_j], blk)
        lower_products = jnp.einsum('mna,nab->nmb', low[:, glob_i], blk)
        total = total + jax.ops.segment_sum(forward, glob_i, num_segments=nblk)
        total = total + jax.ops.segment_sum(lower_products, glob_j, num_segments=nblk)
        return (total, None)
    start = jnp.zeros((nblk, rows, BLOCK), jnp.float32)
    total, _ = lax.scan(one_row, start, jnp.arange(N_ROW, dtype=jnp.int32))
    return total.transpose(1, 0, 2).reshape(rows, -1)

def upper_products(left, right):
    return jnp.dot(left, right, precision=lax.Precision.HIGHEST, preferred_element_type=jnp.float32)

def reference(x_start, p_start, blocks, block_in_row, col_block, coefs):
    k = STATES_K
    both = apply_h(jnp.concatenate([x_start, p_start], 0), blocks, block_in_row, col_block)
    xs, ps = (x_start, p_start)
    hx, hp = (both[:k], both[k:])
    for step in range(ITERS):
        quot = upper_products(xs, hx.T)
        resid = hx - upper_products(quot.T, xs)
        hr = apply_h(resid, blocks, block_in_row, col_block)
        space = jnp.concatenate([xs, resid, ps], 0)
        images = jnp.concatenate([hx, hr, hp], 0)
        gram = upper_products(space, space.T)
        coef = coefs[step]
        coef_p = jnp.concatenate([jnp.zeros((k, k), jnp.float32), coef[k:]], 0)
        norm_x = jnp.diag(upper_products(coef.T, upper_products(gram, coef)))
        norm_p = jnp.diag(upper_products(coef_p.T, upper_products(gram, coef_p)))
        scale_x = 1.0 / jnp.sqrt(norm_x)[:, None]
        scale_p = 1.0 / jnp.sqrt(norm_p)[:, None]
        xs = upper_products(coef.T, space) * scale_x
        hx = upper_products(coef.T, images) * scale_x
        ps = upper_products(coef_p.T, space) * scale_p
        hp = upper_products(coef_p.T, images) * scale_p
    return xs
```

```python
import jax
import jax.numpy as jnp
from jax import lax
from jax.experimental import pallas as pl
from jax.experimental.pallas import tpu as pltpu
from jax.sharding import PartitionSpec as P

MESH = pl.DeviceIdType.MESH
HI = lax.Precision.HIGHEST
F32, BF16 = jnp.float32, jnp.bfloat16
NNZ = 96
PLANE = 32
NCOL = 16
ZLOW = NCOL // 2
ZALL = 2 * ZLOW
UNROLL = 8
NSEM = 48


def dot(a, b, dims, precision=None):
    return lax.dot_general(a, b, (dims, ((), ())), precision=precision, preferred_element_type=F32)


def sort_meta(key_row, other_row, pad_ref):
    lane = lax.broadcasted_iota(jnp.int32, (128, 128), 1).astype(F32)
    sub = lax.broadcasted_iota(jnp.int32, (128, 128), 0).astype(F32)
    pad_ref[...] = jnp.full((8, 128), 1000.0, F32)
    pad_ref[0:1, 0:NNZ] = key_row.astype(F32)
    pad_ref[1:2, 0:NNZ] = other_row.astype(F32)
    key_lane = jnp.broadcast_to(pad_ref[0:1, :], (128, 128))
    other_lane = jnp.broadcast_to(pad_ref[1:2, :], (128, 128))
    key_sub = key_lane.T
    other_sub = other_lane.T
    before = (key_lane < key_sub) | ((key_lane == key_sub) & (lane < sub))
    rank = jnp.sum(jnp.where(before, 1.0, 0.0), axis=1, keepdims=True)
    here = rank == lane
    place = jnp.sum(jnp.where(here, sub, 0.0), axis=0, keepdims=True)
    other = jnp.sum(jnp.where(here, other_sub, 0.0), axis=0, keepdims=True)
    key = jnp.sum(jnp.where(here, key_sub, 0.0), axis=0, keepdims=True)
    earlier = jnp.sum(jnp.where(rank == lane - 1.0, key_sub, 0.0), axis=0, keepdims=True)
    keep = jnp.where(key == earlier, 1.0, 0.0)
    end = jnp.sum(jnp.where(key_sub <= lane, 1.0, 0.0), axis=0, keepdims=True)
    start = jnp.sum(jnp.where(key_sub < lane, 1.0, 0.0), axis=0, keepdims=True)
    last = jnp.where(end > start, end, 0.0)
    return [v.astype(jnp.int32) for v in (place, other, keep, last)]


def gram_tile(basis):
    padded = jnp.concatenate([basis, jnp.zeros((104, 128), F32)], 0)
    g = dot(basis, padded, ((1,), (1,)), HI)
    return g[0:8] + pltpu.roll(g[8:16], 32, 1) + pltpu.roll(g[16:24], 64, 1)


def prepare(row_ref, col_ref, coef_ref, meta_ref, turn_ref, pad_ref):
    rows = row_ref[0]
    cols = col_ref[0]
    for i, v in enumerate(sort_meta(cols, rows, pad_ref) + sort_meta(rows, cols, pad_ref)):
        meta_ref[i:i + 1, :] = v
    k = lax.broadcasted_iota(jnp.int32, (24, 128), 0)
    lane = lax.broadcasted_iota(jnp.int32, (24, 128), 1)
    place = jnp.where(k < 8, k, jnp.where(k < 16, k + 8, k - 8))
    for i in range(2):
        turn_ref[i, 0] = dot(coef_ref[i], jnp.where(lane == place, 1.0, 0.0).astype(F32), ((0,), (0,)), HI)
        only = (lane == k - 8) & (k >= 8) & (k < 16)
        turn_ref[i, 1] = dot(coef_ref[i], jnp.where(only, 1.0, 0.0).astype(F32), ((0,), (0,)), HI)


def rotation(ct, cb, tile):
    lane8 = lax.broadcasted_iota(jnp.int32, (8, 128), 1)
    hx_rows = pltpu.roll(tile, 64, 1)
    at = jnp.where(lane8 < 8, hx_rows, 0.0)
    back = dot(cb[:, 0:8], at, ((1,), (0,)), HI)
    t = ct - back
    tp = jnp.where(lane8 < 8, 0.0, ct) - back
    gam = jnp.concatenate([tile, pltpu.roll(tile, 96, 1), hx_rows], 0)
    both = jnp.concatenate([t, tp], 0)
    norm = jnp.sum(dot(both[:, 0:24], gam, ((1,), (0,)), HI) * both, axis=1, keepdims=True)
    return both, 1.0 / jnp.sqrt(norm)


def kernel(x_ref, p_ref, blk_hbm, meta, turn_ref, o_ref,
           blk, vs, vr1, vr2, vc1, vc2, prefix, cp1, cp2, rp1, rp2, rs1, rs2, cr1, cr2, zs, zr,
           gs, gr, gp, gz, sems):
    r = lax.axis_index("row")
    c = lax.axis_index("col")
    zh = r // PLANE
    p = lax.rem(r, PLANE)
    zl = c // 2
    core = lax.rem(c, 2)
    zi = zh * ZLOW + zl
    other_core = zl * 2 + 1 - core
    other_r = (1 - zh) * PLANE + p

    def copy(src, dst, send, recv, dev):
        return pltpu.make_async_remote_copy(
            src_ref=src, dst_ref=dst, send_sem=sems.at[send], recv_sem=sems.at[recv], device_id=dev, device_id_type=MESH
        )

    def arrived(ref, sem):
        copy(ref, ref, NSEM - 1, sem, (r, other_core)).wait_recv()

    def left(ref, sem):
        copy(ref, ref, sem, NSEM - 1, (r, other_core)).wait_send()

    def plane_send(src, dst, send, recv):
        def step(i, _):
            q = lax.rem(p + i, PLANE)
            copy(src(q), dst, send, recv, (zh * PLANE + q, c)).start()
            return 0

        lax.fori_loop(1, PLANE, step, 0)

    def col_send(src, dst, send, recv):
        def step(i, _):
            q = lax.rem(c + i, NCOL)
            copy(src(q), dst, send, recv, (r, q)).start()
            return 0

        lax.fori_loop(1, NCOL, step, 0)

    def z_send(src, dst, send, recv):
        def step(i, _):
            q = lax.rem(zi + i, ZALL)
            copy(src, dst, send, recv, (q // ZLOW * PLANE + p, lax.rem(q, ZLOW) * 2 + core)).start()
            return 0

        lax.fori_loop(1, ZALL, step, 0)

    bar = pltpu.get_barrier_semaphore()

    def greet_plane(i, _):
        pl.semaphore_signal(bar, 1, device_id=(zh * PLANE + lax.rem(p + i, PLANE), c), device_id_type=MESH)
        return 0

    def greet_col(i, _):
        pl.semaphore_signal(bar, 1, device_id=(r, lax.rem(c + i, NCOL)), device_id_type=MESH)
        return 0

    def greet_far(i, _):
        pl.semaphore_signal(bar, 1, device_id=(other_r, i * 2 + core), device_id_type=MESH)
        return 0

    lax.fori_loop(0, ZLOW, greet_far, 0)
    lax.fori_loop(1, NCOL, greet_col, 0)
    lax.fori_loop(1, PLANE, greet_plane, 0)

    load = pltpu.make_async_copy(blk_hbm.at[0, 0], blk, sems.at[0])
    load.start()
    x = x_ref[...]
    d = p_ref[...]
    vs[0] = jnp.concatenate([x, d], 0).astype(BF16)

    @pl.when(zh == 1)
    def _():
        vc1[0:PLANE] = jnp.zeros((PLANE, 16, 128), BF16)
        vc2[0:PLANE] = jnp.zeros((PLANE, 16, 128), BF16)

    prefix[0] = jnp.zeros((16, 128), F32)
    pl.semaphore_wait(bar, PLANE - 1 + NCOL - 1 + ZLOW)

    def products(v_ref, base, transposed, half):
        dims = ((1,), (1,)) if transposed else ((1,), (0,))
        m = 8 if half else 16

        def step(it, total):
            for u in range(UNROLL):
                k = it * UNROLL + u
                part = dot(v_ref[meta[base + 1, k]], blk[meta[base, k]], dims)
                if half:
                    part = part[0:8] + part[8:16]
                total = total * meta[base + 2, k].astype(F32) + part
                prefix[k + 1, 0:m] = total
            return total

        lax.fori_loop(0, NNZ // UNROLL, step, jnp.zeros((m, 128), F32))

    def apply_h(ph, sem, hooks):
        half = ph == 1
        v = vs.at[ph]
        vr, vc = (vr2, vc2) if half else (vr1, vc1)

        @pl.when(zh == 1)
        def _():
            copy(v, vc.at[r], sem + 1, sem, (p, c)).start()

        col_send(lambda q: v, vr.at[c], sem + 3, sem + 2)
        plane_send(lambda q: v, vc.at[r], sem + 5, sem + 4)
        vr[c] = vs[ph]
        vc[r] = vs[ph]
        hooks[0]()

        @pl.when(zh == 0)
        def _():
            arrived(vc.at[other_r], sem)
            plane_send(lambda q: vc.at[other_r], vc.at[other_r], sem + 7, sem + 6)

        hooks[1]()
        arrived(vr.at[pl.ds(0, NCOL - 1)], sem + 2)
        if ph == 0:
            load.wait()
        products(vr, 0, False, half)
        if half:
            for q in range(PLANE):
                cp2[q] = jnp.concatenate([prefix[meta[3, q], 0:8], prefix[meta[3, q + PLANE], 0:8]], 0).astype(BF16)
            plane_send(lambda q: cp2.at[q], rs2.at[p], sem + 9, sem + 8)
            rs2[p] = cp2[p]
        else:
            for q in range(PLANE):
                cp1[q, 0] = prefix[meta[3, q]].astype(BF16)
                cp1[q, 1] = prefix[meta[3, q + PLANE]].astype(BF16)

            @pl.when(zh == 0)
            def _():
                plane_send(lambda q: cp1.at[q], rs1.at[p], sem + 9, sem + 8)

            @pl.when(zh == 1)
            def _():
                plane_send(lambda q: cp1.at[q, 1], rs1.at[p, 1], sem + 9, sem + 8)

            rs1[p] = cp1[p]

        arrived(vc.at[pl.ds(0, PLANE - 1)], sem + 4)

        @pl.when(zh == 0)
        def _():
            arrived(vc.at[pl.ds(0, PLANE - 1)], sem + 6)

        products(vc, 4, True, half)
        m = 8 if half else 16
        rp, cr = (rp2, cr2) if half else (rp1, cr1)
        for q in range(NCOL):
            rp[q] = prefix[meta[7, q], 0:m].astype(rp.dtype)
        col_send(lambda q: rp.at[q], cr.at[c], sem + 11, sem + 10)
        cr[c] = rp[c]
        hooks[2]()

        if half:
            arrived(rs2.at[pl.ds(0, PLANE - 1)], sem + 8)
            total = jnp.sum(rs2[...].astype(F32), axis=0)
            near, far = total[0:8], total[8:16]
        else:
            @pl.when(zh == 0)
            def _():
                arrived(rs1.at[pl.ds(0, PLANE - 1)], sem + 8)

            @pl.when(zh == 1)
            def _():
                arrived(rs1.at[pl.ds(0, PLANE - 1), 1], sem + 8)

            far = jnp.sum(rs1[:, 1].astype(F32), axis=0)

        z_out, z_in = zs.at[ph, pl.ds(0, m)], zr.at[ph, pl.ds(0, m)]
        zs[ph, 0:m] = far

        @pl.when(zh == 0)
        def _():
            copy(z_out, z_in, sem + 13, sem + 12, (other_r, c)).start()
            if half:
                zr[ph, 0:m] = near
            else:
                zr[ph, 0:m] = jnp.sum(rs1[:, 0].astype(F32), axis=0)

        hooks[3]()
        arrived(cr.at[pl.ds(0, NCOL - 1)], sem + 10)
        total = jnp.sum(cr[...].astype(F32), axis=0)

        @pl.when(zh == 1)
        def _():
            arrived(z_in, sem + 12)

        result = total + zr[ph, 0:m] + jnp.where(zh == 1, 1.0, 0.0) * zs[ph, 0:m]

        def drain():
            left(vr.at[pl.ds(0, NCOL - 1)], sem + 3)
            left(vc.at[pl.ds(0, PLANE - 1)], sem + 5)
            left(rp.at[pl.ds(0, NCOL - 1)], sem + 11)
            if half:
                left(cp2.at[pl.ds(0, PLANE - 1)], sem + 9)

            @pl.when(zh == 0)
            def _():
                left(vc.at[pl.ds(0, PLANE - 1)], sem + 7)
                if not half:
                    left(cp1.at[pl.ds(0, PLANE - 1)], sem + 9)
                left(z_out, sem + 13)

            @pl.when(zh == 1)
            def _():
                left(vs.at[ph], sem + 1)
                if not half:
                    left(cp1.at[pl.ds(0, PLANE - 1), 1], sem + 9)

        return result, drain

    def reduce_steps(k, sem):
        def first(tile):
            gs[k] = tile
            copy(gs.at[k], gr.at[k], sem + 1, sem, (r, other_core)).start()

        def second():
            arrived(gr.at[k], sem)
            gp[k, p] = gs[k] + gr[k]
            plane_send(lambda q: gp.at[k, p], gp.at[k, p], sem + 3, sem + 2)

        def third():
            arrived(gp.at[k, pl.ds(0, PLANE - 1)], sem + 2)
            gz[k, zi] = jnp.sum(gp[k], axis=0)
            z_send(gz.at[k, zi], gz.at[k, zi], sem + 5, sem + 4)

        def fourth():
            arrived(gz.at[k, pl.ds(0, ZALL - 1)], sem + 4)
            return jnp.sum(gz[k], axis=0)

        def drain():
            left(gs.at[k], sem + 1)
            left(gp.at[k, pl.ds(0, PLANE - 1)], sem + 3)
            left(gz.at[k, pl.ds(0, ZALL - 1)], sem + 5)

        return first, second, third, fourth, drain

    def nothing():
        return None

    both, drain1 = apply_h(0, 2, [nothing] * 4)
    hx, hp = both[0:8], both[8:16]
    high = hx.astype(BF16)
    vs[1] = jnp.concatenate([hx, hx - high.astype(F32)], 0).astype(BF16)
    first, second, third, fourth, drain3 = reduce_steps(0, 30)
    basis = jnp.concatenate([x, d, hx], 0)
    early = {}

    def hook0():
        first(gram_tile(basis))

    def hook3():
        rot, scale = rotation(turn_ref[0, 0], turn_ref[0, 1], fourth())
        early["xp"] = dot(rot[:, 0:24], basis, ((1,), (0,)), HI) * scale
        early["rot"], early["scale"] = rot, scale

    hhx, drain2 = apply_h(1, 16, [hook0, second, third, hook3])
    xp, rot, scale = early["xp"], early["rot"], early["scale"]
    image = dot(rot[0:8, 0:24], jnp.concatenate([hx, hp, hhx], 0), ((1,), (0,)), HI) * scale[0:8]
    basis2 = jnp.concatenate([xp, image], 0)
    first, second, third, fourth, drain4 = reduce_steps(1, 36)
    first(gram_tile(basis2))
    second()
    third()
    drain1()
    drain2()
    drain3()
    rot2, scale2 = rotation(turn_ref[1, 0], turn_ref[1, 1], fourth())
    o_ref[...] = dot(rot2[0:8, 0:24], basis2, ((1,), (0,)), HI) * scale2[0:8]
    drain4()


def body(x_start, p_start, blocks, block_in_row, col_block, coefs):
    vmem = pl.BlockSpec(memory_space=pltpu.VMEM)
    meta, turn = pl.pallas_call(
        prepare,
        out_shape=(jax.ShapeDtypeStruct((8, 128), jnp.int32), jax.ShapeDtypeStruct((2, 2, 8, 128), F32)),
        in_specs=[vmem] * 3,
        out_specs=(vmem, vmem),
        scratch_shapes=[pltpu.VMEM((8, 128), F32)],
        name="prepare",
    )(block_in_row, col_block, coefs)
    return pl.pallas_call(
        kernel,
        out_shape=jax.ShapeDtypeStruct((8, 128), F32),
        in_specs=[vmem, vmem, pl.BlockSpec(memory_space=pl.ANY), pl.BlockSpec(memory_space=pltpu.SMEM), vmem],
        out_specs=vmem,
        scratch_shapes=[
            pltpu.VMEM((NNZ, 128, 128), BF16),
            pltpu.VMEM((2, 16, 128), BF16),
            pltpu.VMEM((NCOL, 16, 128), BF16),
            pltpu.VMEM((NCOL, 16, 128), BF16),
            pltpu.VMEM((2 * PLANE, 16, 128), BF16),
            pltpu.VMEM((2 * PLANE, 16, 128), BF16),
            pltpu.VMEM((NNZ + 1, 16, 128), F32),
            pltpu.VMEM((PLANE, 2, 16, 128), BF16),
            pltpu.VMEM((PLANE, 16, 128), BF16),
            pltpu.VMEM((NCOL, 16, 128), BF16),
            pltpu.VMEM((NCOL, 8, 128), F32),
            pltpu.VMEM((PLANE, 2, 16, 128), BF16),
            pltpu.VMEM((PLANE, 16, 128), BF16),
            pltpu.VMEM((NCOL, 16, 128), BF16),
            pltpu.VMEM((NCOL, 8, 128), F32),
            pltpu.VMEM((2, 16, 128), F32),
            pltpu.VMEM((2, 16, 128), F32),
            pltpu.VMEM((2, 8, 128), F32),
            pltpu.VMEM((2, 8, 128), F32),
            pltpu.VMEM((2, PLANE, 8, 128), F32),
            pltpu.VMEM((2, ZALL, 8, 128), F32),
            pltpu.SemaphoreType.DMA((NSEM,)),
        ],
        compiler_params=pltpu.CompilerParams(
            collective_id=0, has_side_effects=True, vmem_limit_bytes=32 * 1024 * 1024
        ),
        name="lobpcg",
    )(x_start, p_start, blocks, meta, turn)


def solution(mesh):
    return jax.shard_map(
        body,
        mesh=mesh,
        in_specs=(
            P(None, ("row", "col")),
            P(None, ("row", "col")),
            P("row", "col", None, None, None),
            P("row", "col", None),
            P("row", "col", None),
            P(),
        ),
        out_specs=P(None, ("row", "col")),
        check_vma=False,
    )
```

```python
import jax
import jax.numpy as jnp
from jax import lax
from jax.experimental import pallas as pl
from jax.experimental.pallas import tpu as pltpu
from jax.sharding import PartitionSpec as P

MESH = pl.DeviceIdType.MESH
HI = lax.Precision.HIGHEST
F32, BF16 = jnp.float32, jnp.bfloat16
NNZ = 96
PLANE = 32
NCOL = 16
ZLOW = NCOL // 2
ZALL = 2 * ZLOW
UNROLL = 48
NSEM = 52


def dot(a, b, dims, precision=None):
    return lax.dot_general(a, b, (dims, ((), ())), precision=precision, preferred_element_type=F32)


def sort_meta(key_row, other_row, pad_ref):
    lane = lax.broadcasted_iota(jnp.int32, (128, 128), 1)
    sub = lax.broadcasted_iota(jnp.int32, (128, 128), 0)
    pad_ref[...] = jnp.full((8, 128), 1000, jnp.int32)
    pad_ref[0:1, 0:NNZ] = key_row
    pad_ref[1:2, 0:NNZ] = other_row
    key_lane = jnp.broadcast_to(pad_ref[0:1, :], (128, 128))
    other_lane = jnp.broadcast_to(pad_ref[1:2, :], (128, 128))
    key_sub = key_lane.T
    other_sub = other_lane.T
    before = (key_lane < key_sub) | ((key_lane == key_sub) & (lane < sub))
    rank = jnp.sum(jnp.where(before, 1, 0), axis=1, keepdims=True)
    here = rank == lane
    place = jnp.sum(jnp.where(here, sub, 0), axis=0, keepdims=True)
    other = jnp.sum(jnp.where(here, other_sub, 0), axis=0, keepdims=True)
    key = jnp.sum(jnp.where(here, key_sub, 0), axis=0, keepdims=True)
    earlier = jnp.sum(jnp.where(rank == lane - 1, key_sub, 0), axis=0, keepdims=True)
    keep = jnp.where(key == earlier, 1, 0)
    end = jnp.sum(jnp.where(key_sub <= lane, 1, 0), axis=0, keepdims=True)
    start = jnp.sum(jnp.where(key_sub < lane, 1, 0), axis=0, keepdims=True)
    last = jnp.where(end > start, end, 0)
    return place, other, keep, last


SHIFTS = (0, 32, 56, 72, 80)


def gram_tile(basis):
    padded = jnp.concatenate([basis, jnp.zeros((88, 128), F32)], 0)
    g = dot(basis, padded, ((1,), (1,)), HI)
    lane = lax.broadcasted_iota(jnp.int32, (8, 128), 1)
    tile = g[0:8]
    for i in range(1, 5):
        tile += pltpu.roll(jnp.where(lane >= 8 * i, g[8 * i:8 * i + 8], 0.0), SHIFTS[i], 1)
    return tile


def gram_full(tile):
    lane = lax.broadcasted_iota(jnp.int32, (8, 128), 1)
    upper, strict = [], []
    for i in range(5):
        part = tile if i == 0 else pltpu.roll(tile, 128 - SHIFTS[i], 1)
        upper.append(jnp.where((lane >= 8 * i) & (lane < 40), part, 0.0))
        strict.append(jnp.where((lane >= 8 * i + 8) & (lane < 40), part, 0.0))
    rest = [jnp.zeros((88, 128), F32)]
    return jnp.concatenate(upper + rest, 0) + jnp.concatenate(strict + rest, 0).T


def turns(coef_t):
    k = lax.broadcasted_iota(jnp.int32, (24, 128), 0)
    lane = lax.broadcasted_iota(jnp.int32, (24, 128), 1)
    place = jnp.where(k < 8, k, jnp.where(k < 16, k + 8, k - 8))
    only = (lane == k - 8) & (k >= 8) & (k < 16)
    ct = dot(coef_t, jnp.where(lane == place, 1.0, 0.0).astype(F32), ((1,), (0,)), HI)
    cb = dot(coef_t, jnp.where(only, 1.0, 0.0).astype(F32), ((1,), (0,)), HI)
    return ct, cb


def rotation(turn, gram):
    ct, cb = turn
    lane = lax.broadcasted_iota(jnp.int32, (8, 128), 1)
    at = jnp.where(lane < 8, gram[16:24], 0.0)
    back = dot(cb[:, 0:8], at, ((1,), (0,)), HI)
    both = jnp.concatenate([ct - back, jnp.where(lane < 8, 0.0, ct) - back], 0)
    norm = jnp.sum(dot(both[:, 0:24], gram[0:24], ((1,), (0,)), HI) * both, axis=1, keepdims=True)
    return both, 1.0 / jnp.sqrt(norm)


def kernel(x_hbm, p_hbm, blk_hbm, row_hbm, col_hbm, coef_hbm, o_ref,
           x_ref, p_ref, coef_ref, row_ref, col_ref, pad, meta_v, meta, blk, vs, vr1, vr2, vc1, vc2, prefix, cp1, cp2, rp1, rp2, sb1, sb2, st1, st2, rs1, rs2, cr1, cr2, zs, zr,
           gs, gr, gp, gz, sems):
    r = lax.axis_index("row")
    c = lax.axis_index("col")
    zh = r // PLANE
    p = lax.rem(r, PLANE)
    zl = c // 2
    core = lax.rem(c, 2)
    zi = zh * ZLOW + zl
    ci = core * ZLOW + zl
    mine = pl.ds(core * ZLOW, ZLOW)
    others = pl.ds((1 - core) * ZLOW, ZLOW)
    other_core = zl * 2 + 1 - core
    other_r = (1 - zh) * PLANE + p

    def copy(src, dst, send, recv, dev):
        return pltpu.make_async_remote_copy(
            src_ref=src, dst_ref=dst, send_sem=sems.at[send], recv_sem=sems.at[recv], device_id=dev, device_id_type=MESH
        )

    def arrived(ref, sem):
        copy(ref, ref, NSEM - 1, sem, (r, other_core)).wait_recv()

    def left(ref, sem):
        copy(ref, ref, sem, NSEM - 1, (r, other_core)).wait_send()

    def plane_send(src, dst, send, recv):
        def step(i, _):
            q = lax.rem(p + i, PLANE)
            copy(src(q), dst, send, recv, (zh * PLANE + q, c)).start()
            return 0

        lax.fori_loop(1, PLANE, step, 0)

    def col_send(src, dst, send, recv):
        def step(i, _):
            q = lax.rem(zl + i, ZLOW)
            copy(src(q), dst, send, recv, (r, q * 2 + core)).start()
            return 0

        lax.fori_loop(1, ZLOW, step, 0)

    def z_send(src, dst, send, recv):
        def step(i, _):
            q = lax.rem(zi + i, ZALL)
            copy(src, dst, send, recv, (q // ZLOW * PLANE + p, lax.rem(q, ZLOW) * 2 + core)).start()
            return 0

        lax.fori_loop(1, ZALL, step, 0)

    bar = pltpu.get_barrier_semaphore()

    def greet_plane(i, _):
        pl.semaphore_signal(bar, 1, device_id=(zh * PLANE + lax.rem(p + i, PLANE), c), device_id_type=MESH)
        return 0

    def greet_col(i, _):
        pl.semaphore_signal(bar, 1, device_id=(r, lax.rem(zl + i, ZLOW) * 2 + core), device_id_type=MESH)
        return 0

    def greet_far(i, _):
        pl.semaphore_signal(bar, 1, device_id=(other_r, i * 2 + core), device_id_type=MESH)
        return 0

    lax.fori_loop(0, ZLOW, greet_far, 0)
    lax.fori_loop(1, ZLOW, greet_col, 0)
    pl.semaphore_signal(bar, 1, device_id=(r, other_core), device_id_type=MESH)
    lax.fori_loop(1, PLANE, greet_plane, 0)

    small = [
        pltpu.make_async_copy(src, dst, sems.at[n])
        for src, dst, n in (
            (row_hbm, row_ref, 49), (col_hbm, col_ref, 50), (x_hbm, x_ref, 1), (p_hbm, p_ref, 46), (coef_hbm, coef_ref, 47)
        )
    ]
    for one in small:
        one.start()
    load = pltpu.make_async_copy(blk_hbm.at[0, 0], blk, sems.at[0])
    load.start()
    for one in small:
        one.wait()
    x = x_ref[...]
    d = p_ref[...]
    vs[0] = jnp.concatenate([x, d], 0).astype(BF16)

    @pl.when(zh == 1)
    def _():
        vc1[0:PLANE] = jnp.zeros((PLANE, 16, 128), BF16)
        vc2[0:PLANE] = jnp.zeros((PLANE, 16, 128), BF16)

    prefix[0] = jnp.zeros((16, 128), F32)
    rows = row_ref[0]
    rows = lax.rem(rows, 2) * ZLOW + rows // 2
    cols = col_ref[0]
    for i, v in enumerate(sort_meta(cols, rows, pad) + sort_meta(rows, cols, pad)):
        meta_v[i:i + 1, :] = v
    tables = pltpu.make_async_copy(meta_v, meta, sems.at[48])
    tables.start()
    tables.wait()
    turn1, turn2 = turns(coef_ref[0]), turns(coef_ref[1])
    pl.semaphore_wait(bar, PLANE - 1 + ZLOW - 1 + 1 + ZLOW)

    def products(v_ref, base, transposed, half):
        dims = ((1,), (1,)) if transposed else ((1,), (0,))
        m = 8 if half else 16

        def step(it, total):
            for u in range(UNROLL):
                k = it * UNROLL + u
                part = dot(v_ref[meta[base + 1, k]], blk[meta[base, k]], dims)
                if half:
                    part = part[0:8] + part[8:16]
                total = total * meta[base + 2, k].astype(F32) + part
                prefix[k + 1, 0:m] = total
            return total

        lax.fori_loop(0, NNZ // UNROLL, step, jnp.zeros((m, 128), F32))

    def apply_h(ph, sem):
        half = ph == 1
        v = vs.at[ph]
        vr, vc = (vr2, vc2) if half else (vr1, vc1)

        @pl.when(zh == 1)
        def _():
            copy(v, vc.at[r], sem + 1, sem, (p, c)).start()

        col_send(lambda q: v, vr.at[ci], sem + 3, sem + 2)
        plane_send(lambda q: v, vc.at[r], sem + 5, sem + 4)
        vr[ci] = vs[ph]
        vc[r] = vs[ph]
        arrived(vr.at[pl.ds(0, ZLOW - 1)], sem + 2)
        copy(vr.at[mine], vr.at[mine], sem + 15, sem + 14, (r, other_core)).start()

        @pl.when(zh == 0)
        def _():
            arrived(vc.at[other_r], sem)
            plane_send(lambda q: vc.at[other_r], vc.at[other_r], sem + 7, sem + 6)

        arrived(vr.at[others], sem + 14)
        if ph == 0:
            load.wait()
        products(vr, 0, False, half)
        if half:
            for q in range(PLANE):
                cp2[q] = jnp.concatenate([prefix[meta[3, q], 0:8], prefix[meta[3, q + PLANE], 0:8]], 0).astype(BF16)
            plane_send(lambda q: cp2.at[q], rs2.at[p], sem + 9, sem + 8)
            rs2[p] = cp2[p]
        else:
            for q in range(PLANE):
                cp1[q, 0] = prefix[meta[3, q]]
                cp1[q, 1] = prefix[meta[3, q + PLANE]]

            plane_send(lambda q: cp1.at[q, 1], rs1.at[p, 1], sem + 9, sem + 8)
            rs1[p] = cp1[p]

        arrived(vc.at[pl.ds(0, PLANE - 1)], sem + 4)

        @pl.when(zh == 0)
        def _():
            arrived(vc.at[pl.ds(0, PLANE - 1)], sem + 6)

        products(vc, 4, True, half)
        m = 8 if half else 16
        rp, sb, st, cr = (rp2, sb2, st2, cr2) if half else (rp1, sb1, st1, cr1)
        for q in range(NCOL):
            rp[q] = prefix[meta[7, q], 0:m]
        copy(rp.at[others], sb, sem + 17, sem + 16, (r, other_core)).start()
        arrived(sb, sem + 16)
        st[...] = (rp[mine] + sb[...]).astype(st.dtype)
        col_send(lambda q: st.at[q], cr.at[zl], sem + 11, sem + 10)
        cr[zl] = st[zl]
        if not half:
            @pl.when(zh == 0)
            def _():
                plane_send(lambda q: cp1.at[q, 0], rs1.at[p, 0], 45, 44)


        if half:
            arrived(rs2.at[pl.ds(0, PLANE - 1)], sem + 8)
            total = jnp.sum(rs2[...].astype(F32), axis=0)
            near, far = total[0:8], total[8:16]
        else:
            arrived(rs1.at[pl.ds(0, PLANE - 1), 1], sem + 8)
            far = jnp.sum(rs1[:, 1].astype(F32), axis=0)

        z_out, z_in = zs.at[ph, pl.ds(0, m)], zr.at[ph, pl.ds(0, m)]
        zs[ph, 0:m] = far

        @pl.when(zh == 0)
        def _():
            copy(z_out, z_in, sem + 13, sem + 12, (other_r, c)).start()
            if half:
                zr[ph, 0:m] = near
            else:
                arrived(rs1.at[pl.ds(0, PLANE - 1), 0], 44)
                zr[ph, 0:m] = jnp.sum(rs1[:, 0].astype(F32), axis=0)

        arrived(cr.at[pl.ds(0, ZLOW - 1)], sem + 10)
        total = jnp.sum(cr[...].astype(F32), axis=0)

        @pl.when(zh == 1)
        def _():
            arrived(z_in, sem + 12)

        result = total + zr[ph, 0:m] + jnp.where(zh == 1, 1.0, 0.0) * zs[ph, 0:m]

        def drain():
            left(vr.at[pl.ds(0, ZLOW - 1)], sem + 3)
            left(vr.at[mine], sem + 15)
            left(sb, sem + 17)
            left(vc.at[pl.ds(0, PLANE - 1)], sem + 5)
            left(st.at[pl.ds(0, ZLOW - 1)], sem + 11)
            left(cp2.at[pl.ds(0, PLANE - 1)] if half else cp1.at[pl.ds(0, PLANE - 1), 1], sem + 9)

            @pl.when(zh == 0)
            def _():
                left(vc.at[pl.ds(0, PLANE - 1)], sem + 7)
                if not half:
                    left(cp1.at[pl.ds(0, PLANE - 1), 0], 45)
                left(z_out, sem + 13)

            @pl.when(zh == 1)
            def _():
                left(vs.at[ph], sem + 1)

        return result, drain

    both, drain1 = apply_h(0, 2)
    hx, hp = both[0:8], both[8:16]
    high = hx.astype(BF16)
    vs[1] = jnp.concatenate([hx, hx - high.astype(F32)], 0).astype(BF16)
    hhx, drain2 = apply_h(1, 20)

    basis = jnp.concatenate([x, d, hx, hp, hhx], 0)
    gs[...] = gram_tile(basis)
    copy(gs, gr, 39, 38, (r, other_core)).start()
    arrived(gr, 38)
    gp[p] = gs[...] + gr[...]
    plane_send(lambda q: gp.at[p], gp.at[p], 41, 40)
    arrived(gp.at[pl.ds(0, PLANE - 1)], 40)
    gz[zi] = jnp.sum(gp[...], axis=0)
    z_send(gz.at[zi], gz.at[zi], 43, 42)
    drain1()
    drain2()
    left(gs, 39)
    left(gp.at[pl.ds(0, PLANE - 1)], 41)
    arrived(gz.at[pl.ds(0, ZALL - 1)], 42)
    gram = gram_full(jnp.sum(gz[...], axis=0))

    rot, scale = rotation(turn1, gram)
    new = rot * scale
    new = jnp.concatenate([new, pltpu.roll(new[0:8], 16, 1)], 0)
    padded = jnp.concatenate([new, jnp.zeros((104, 128), F32)], 0)
    gram2 = dot(dot(new, gram, ((1,), (0,)), HI), padded, ((1,), (1,)), HI)
    rot2, scale2 = rotation(turn2, gram2)
    final = dot(rot2[0:8, 0:24], new, ((1,), (0,)), HI) * scale2[0:8]
    o_ref[...] = dot(final[:, 0:40], basis, ((1,), (0,)), HI)
    left(gz.at[pl.ds(0, ZALL - 1)], 43)


def body(x_start, p_start, blocks, block_in_row, col_block, coefs):
    vmem = pl.BlockSpec(memory_space=pltpu.VMEM)
    hbm = pl.BlockSpec(memory_space=pltpu.HBM)
    limit = 56 * 1024 * 1024
    return pl.pallas_call(
        kernel,
        out_shape=jax.ShapeDtypeStruct((8, 128), F32),
        in_specs=[hbm] * 6,
        out_specs=vmem,
        scratch_shapes=[
            pltpu.VMEM((8, 128), F32),
            pltpu.VMEM((8, 128), F32),
            pltpu.VMEM((2, 8, 24), F32),
            pltpu.VMEM((1, 1, NNZ), jnp.int32),
            pltpu.VMEM((1, 1, NNZ), jnp.int32),
            pltpu.VMEM((8, 128), jnp.int32),
            pltpu.VMEM((8, 128), jnp.int32),
            pltpu.SMEM((8, 128), jnp.int32),
            pltpu.VMEM((NNZ, 128, 128), BF16),
            pltpu.VMEM((2, 16, 128), BF16),
            pltpu.VMEM((NCOL, 16, 128), BF16),
            pltpu.VMEM((NCOL, 16, 128), BF16),
            pltpu.VMEM((2 * PLANE, 16, 128), BF16),
            pltpu.VMEM((2 * PLANE, 16, 128), BF16),
            pltpu.VMEM((NNZ + 1, 16, 128), F32),
            pltpu.VMEM((PLANE, 2, 16, 128), F32),
            pltpu.VMEM((PLANE, 16, 128), BF16),
            pltpu.VMEM((NCOL, 16, 128), F32),
            pltpu.VMEM((NCOL, 8, 128), F32),
            pltpu.VMEM((ZLOW, 16, 128), F32),
            pltpu.VMEM((ZLOW, 8, 128), F32),
            pltpu.VMEM((ZLOW, 16, 128), F32),
            pltpu.VMEM((ZLOW, 8, 128), F32),
            pltpu.VMEM((PLANE, 2, 16, 128), F32),
            pltpu.VMEM((PLANE, 16, 128), BF16),
            pltpu.VMEM((ZLOW, 16, 128), F32),
            pltpu.VMEM((ZLOW, 8, 128), F32),
            pltpu.VMEM((2, 16, 128), F32),
            pltpu.VMEM((2, 16, 128), F32),
            pltpu.VMEM((8, 128), F32),
            pltpu.VMEM((8, 128), F32),
            pltpu.VMEM((PLANE, 8, 128), F32),
            pltpu.VMEM((ZALL, 8, 128), F32),
            pltpu.SemaphoreType.DMA((NSEM,)),
        ],
        compiler_params=pltpu.CompilerParams(
            collective_id=0, has_side_effects=True, vmem_limit_bytes=limit
        ),
        name="lobpcg",
    )(x_start, p_start, blocks, block_in_row, col_block, jnp.transpose(coefs, (0, 2, 1)))


def solution(mesh):
    return jax.shard_map(
        body,
        mesh=mesh,
        in_specs=(
            P(None, ("row", "col")),
            P(None, ("row", "col")),
            P("row", "col", None, None, None),
            P("row", "col", None),
            P("row", "col", None),
            P(),
        ),
        out_specs=P(None, ("row", "col")),
        check_vma=False,
    )
```
